512 devices in a mesh: wide: 128 (over y, z, core), narrow: 4 (over x).
Axes of the slice: x: 4, y: 4, z: 16, core: 2. Of those that a mesh axis runs over, the one named last changes fastest.
Arguments:
- node_factors: float32 [524288, 512], P(('wide', 'narrow')), may hold values from -0.25 to 0.25
- leaf_q: float32 [262144, 512], P(('wide', 'narrow')), may hold values from -0.25 to 0.25
- modal_basis: float32 [512, 64], replicated, may hold values from -6 to 6
Outputs:
- trunk_modes: float32 [262144, 64], P(('wide', 'narrow'))
The draws below stay inside these ranges and needn't reach their ends.
All inputs are finite; a program needn't handle non-finite values.
Results may differ from the reference program's by a relative error of at most 0.0002.
Values sent between devices are 32-bit elements; how exact they have to be, the bound alone decides.
No kernel may reach another device: no remote copies, remote signals or barrier semaphores. Data moves between devices by JAX's collectives and lax.ppermute only.
A program may use at most 64 MiB of HBM per device.

```python
import jax
import jax.numpy as jnp
import numpy as np
from jax import lax

SNAPS = 512
MODES = 64
ROWS_DEV = 512
DEVICES_ALL = 512
LEVELS = 9
ROWS = 262144
N_WIDE = 128
N_NARROW = 4


def steps_of(own_key, extent, pieces, least, top_value):
    level, own = 1.0, jax.random.fold_in(own_key, 6)
    for axis_at, blocks in pieces:
        draws = jnp.exp(jax.random.uniform(jax.random.fold_in(own, axis_at), (blocks,), jnp.float32, least / len(pieces), top_value / len(pieces)))
        level = level * jnp.repeat(draws, extent[axis_at] // blocks).reshape([-1 if axis == axis_at else 1 for axis in range(len(extent))])
    return level


def bell_draw(stream_key, shape, width, reach, cuts=(), held_as=jnp.bfloat16):
    array = width * jax.random.normal(stream_key, shape, jnp.float32)
    if cuts:
        array = array * steps_of(stream_key, shape, cuts, -0.22, 0.18)
    return jnp.clip(array, -reach, reach).astype(held_as)


def setup_inputs(seed: int = 0) -> dict:
    streams_of = jax.random.split(jax.random.key(seed), 4)
    return {
        "node_factors": bell_draw(streams_of[0], (DEVICES_ALL * 2 * SNAPS, SNAPS), SNAPS ** -0.5, 0.25, ((0, 512),), jnp.float32),
        "leaf_q": bell_draw(streams_of[1], (ROWS, SNAPS), SNAPS ** -0.5, 0.25, ((0, 512),), jnp.float32),
        "modal_basis": bell_draw(streams_of[2], (SNAPS, MODES), 1.0, 6.0, (), jnp.float32),
    }


def reference(node_factors, leaf_q, modal_basis):
    leaf_count = N_WIDE * N_NARROW
    blocks = node_factors.reshape(leaf_count, 2 * SNAPS, SNAPS)
    coefficient = modal_basis[None]
    for level in range(LEVELS, 0, -1):
        owners = np.arange(leaf_count >> level) * (2 ** level) + 2 ** (level - 1)
        selected = blocks[owners]
        product = jnp.einsum("nij,njr->nir", selected, coefficient, precision=lax.Precision.HIGHEST)
        coefficient = product.reshape(-1, SNAPS, MODES)
    leaves = leaf_q.reshape(leaf_count, ROWS_DEV, SNAPS)
    result = jnp.einsum("nmk,nkr->nmr", leaves, coefficient, precision=lax.Precision.HIGHEST)
    return result.reshape(-1, MODES)
```

```python
import jax
import jax.numpy as jnp
from jax import lax
from jax.sharding import PartitionSpec as P

AXES = ("wide", "narrow")


def times(coefficient, factor):
    return lax.dot_general(
        coefficient, factor, (((1,), (1,)), ((), ())),
        precision=lax.Precision.HIGH, preferred_element_type=jnp.float32,
    )


def on_device(node_factors, leaf_q, modal_basis):
    leaf_count = lax.axis_size("wide") * lax.axis_size("narrow")
    levels = leaf_count.bit_length() - 1
    snaps = node_factors.shape[1]
    leaf = lax.axis_index("wide") * lax.axis_size("narrow") + lax.axis_index("narrow")
    held = modal_basis.T
    upper, lower = node_factors[:snaps], node_factors[snaps:]
    for level in range(levels, 0, -1):
        reach = 2 ** (level - 1)
        owners = range(reach, leaf_count, 2 * reach)
        left = times(held, upper)
        if level > 1:
            step = reach // 2
            from_right = lax.ppermute(left, AXES, [(o, o - step) for o in owners])
            right = times(held, lower)
            from_left = lax.ppermute(right, AXES, [(o, o + step) for o in owners])
            held = jnp.where(leaf % (4 * step) == step, from_right, from_left)
        else:
            from_right = lax.ppermute(left, AXES, [(o, o - 1) for o in owners])
            right = times(held, lower)
            held = jnp.where(leaf % 2 == 0, from_right, right)
    return times(held, leaf_q).T


def solution(mesh):
    return jax.shard_map(
        on_device,
        mesh=mesh,
        in_specs=(P(AXES, None), P(AXES, None), P()),
        out_specs=P(AXES, None),
        check_vma=False,
    )
```

```python
import functools

import jax
import jax.numpy as jnp
from jax import lax
from jax.experimental import pallas as pl
from jax.experimental.pallas import tpu as pltpu
from jax.sharding import PartitionSpec as P

AXES = ("wide", "narrow")
Y, Z, CORES, X = 4, 16, 2, 4
SNAPS, MODES = 512, 64


def at(y, z, core, x):
    return ((y * Z + z) * CORES + core) * X + x


EVERY = [(y, z, core, x) for y in range(Y) for z in range(Z) for core in range(CORES) for x in range(X)]


def split(value):
    high = value.astype(jnp.bfloat16)
    return high, (value - high.astype(jnp.float32)).astype(jnp.bfloat16)


def times(coefficient, factor):
    dims = (((1,), (1,)), ((), ()))
    c_high, c_low = split(coefficient)
    f_high, f_low = split(factor)
    both = lax.dot_general(
        jnp.concatenate([c_high, c_low], 0), f_high, dims, preferred_element_type=jnp.float32
    )
    cross = lax.dot_general(c_high, f_low, dims, preferred_element_type=jnp.float32)
    return both[:MODES] + (both[MODES:] + cross)


def chain_kernel(plan, pick_ref, *refs):
    n_coefs, steps, ends, n_near, n_far = plan
    coefs, near, far, outs, scratch = (
        refs[sum(plan_sizes[:i]):sum(plan_sizes[:i + 1])]
        for plan_sizes in [(n_coefs, n_near, n_far, len(ends), len(refs) - n_coefs - n_near - n_far - len(ends))]
        for i in range(5)
    )
    held = scratch[0]

    def block(which):
        operand, half = which
        return near[operand][half * SNAPS:(half + 1) * SNAPS, :]

    @pl.when(pick_ref[0] >= 0)
    def _():
        fetches = {}
        for s, choices in enumerate(steps):
            for i, (operand, half) in enumerate(choices):
                if operand >= n_near:
                    fetches[s, i] = pltpu.make_async_copy(
                        far[operand - n_near], scratch[1].at[s], scratch[2].at[s]
                    )
                    pl.when(pick_ref[s + 1] == i)(fetches[s, i].start)
        for i, coef in enumerate(coefs):
            @pl.when(pick_ref[0] == i)
            def _():
                held[...] = coef[...]
        for s, choices in enumerate(steps):
            for i, which in enumerate(choices):
                @pl.when(pick_ref[s + 1] == i)
                def _():
                    if (s, i) in fetches:
                        fetches[s, i].wait()
                        held[...] = times(held[...], scratch[1][s])
                    else:
                        held[...] = times(held[...], block(which))
        for out, which in zip(outs, ends):
            out[...] = held[...] if which is None else times(held[...], block(which))


def chain(picks, coefs, near, far, steps, ends):
    vmem = pl.BlockSpec(memory_space=pltpu.VMEM)
    plan = (len(coefs), tuple(map(tuple, steps)), tuple(ends), len(near), len(far))
    result = jax.ShapeDtypeStruct((MODES, SNAPS), jnp.float32)
    scratch = [pltpu.VMEM((MODES, SNAPS), jnp.float32)]
    if far:
        scratch += [pltpu.VMEM((len(steps), SNAPS, SNAPS), jnp.float32), pltpu.SemaphoreType.DMA((len(steps),))]
    return pl.pallas_call(
        functools.partial(chain_kernel, plan),
        out_shape=[result] * len(ends),
        in_specs=[pl.BlockSpec(memory_space=pltpu.SMEM)] + [vmem] * (len(coefs) + len(near))
        + [pl.BlockSpec(memory_space=pl.ANY)] * len(far),
        out_specs=[vmem] * len(ends),
        scratch_shapes=scratch,
        compiler_params=pltpu.CompilerParams(vmem_limit_bytes=16 << 20),
        cost_estimate=pl.CostEstimate(flops=0, bytes_accessed=0, transcendentals=0),
    )(jnp.stack([jnp.asarray(p, jnp.int32) for p in picks]), *coefs, *near, *far)


def choose(*cases):
    picked = jnp.int32(-1)
    for i in reversed(range(len(cases))):
        picked = jnp.where(cases[i], jnp.int32(i), picked)
    return picked


def send(block, route):
    return lax.ppermute(block, AXES, route)


def on_device(node_factors, leaf_q, modal_basis):
    wide, x = lax.axis_index("wide"), lax.axis_index("narrow")
    core, z, y = wide % CORES, (wide // CORES) % Z, wide // (CORES * Z)
    trunk = (core == 0) & (x == 0)
    U, L = 0, 1

    up, low = chain(
        [choose(trunk & (z == 0) & (y == 2))], [modal_basis.T], [node_factors], [], [], [(0, U), (0, L)]
    )
    to_y1 = send(up, [(at(2, 0, 0, 0), at(1, 0, 0, 0))])
    to_y3 = send(low, [(at(2, 0, 0, 0), at(3, 0, 0, 0))])

    factors, up, low = lax.optimization_barrier((node_factors, up, low))
    upper = factors[:SNAPS]
    other = lax.dynamic_slice_in_dim(factors, jnp.where((core == 1) & (x == 0), 0, SNAPS), SNAPS)
    late = (4, 6, 12)
    early_a = send(
        upper,
        [(at(y, z, c, x), at(y, z, c, x - 1)) for y, z, c, x in EVERY if x >= 2]
        + [(at(y, 8, 0, 0), at(y, 4, 0, 0)) for y in range(Y)]
        + [(at(y, z + 1, 0, 0), at(y, z, 0, 0)) for y in range(Y) for z in range(0, Z, 2) if z not in late]
        + [(at(y, 12, 1, 0), at(y, 12, 0, 0)) for y in range(Y)],
    )
    early_b = send(
        other,
        [(at(y, z, c, 2), at(y, z, c, 3)) for y, z, c, x in EVERY if x == 2]
        + [(at(y, 8, 0, 0), at(y, 12, 0, 0)) for y in range(Y)]
        + [(at(y, z, 1, 0), at(y, z, 0, 0)) for y in range(Y) for z in range(Z) if z != 12],
    )
    early_c = send(upper, [(at(y, z + 1, 0, 0), at(y, z, 0, 0)) for y in range(Y) for z in late])

    up, low = chain(
        [choose(trunk & (z == 0) & (y == 1), trunk & (z == 0) & (y == 3))],
        [to_y1, to_y3], [node_factors], [], [], [(0, U), (0, L)],
    )
    c7 = [
        send(half, [(at(y, 0, 0, 0), at(y - 1 + k, zt, 0, 0)) for y in (1, 3)])
        for k, half in enumerate((up, low)) for zt in (4, 12)
    ]
    *c7, early_a, early_b = lax.optimization_barrier((*c7, early_a, early_b))
    z4, z12, y_low = trunk & (z == 4), trunk & (z == 12), y % 2 == 0
    up, low = chain(
        [choose(z4 & y_low, z12 & y_low, z4 & ~y_low, z12 & ~y_low), choose(z4, z12)],
        c7, [node_factors], [early_a, early_b], [[(1, 0), (2, 0)]], [(0, U), (0, L)],
    )
    c5 = [
        send(half, [(at(y, z, 0, 0), at(y, z + step, 0, 0)) for y in range(Y) for z in (4, 12)])
        for half, step in ((up, -2), (low, 2))
    ]
    up, low = chain(
        [choose(trunk & (z % 8 == 2), trunk & (z % 8 == 6))], c5, [node_factors], [], [], [(0, U), (0, L)]
    )
    c4 = [
        send(half, [(at(y, z, 0, 0), at(y, z + step, 0, 0)) for y in range(Y) for z in range(2, Z, 4)])
        for half, step in ((up, -2), (up, -1), (low, 1))
    ]
    is_late = (z == late[0]) | (z == late[1]) | (z == late[2])
    (c3,) = chain(
        [choose(*[trunk & (z % 4 == k) for k in (0, 1, 3, 2)]), choose(z % 2 == 1, is_late, z % 2 == 0)],
        c4 + [low], [node_factors], [early_a, early_c], [[(0, L), (2, 0), (1, 0)]], [None],
    )
    over = send(c3, [(at(y, z, 0, 0), at(y, z, 1, 0)) for y in range(Y) for z in range(Z)])
    (c2,) = chain(
        [choose((core == 0) & (x == 0), (core == 1) & (x == 0)), choose(core == 1, z == 12, z != 12)],
        [c3, over], [node_factors], [early_a, early_b], [[(0, L), (1, 0), (2, 0)]], [None],
    )
    spread = [
        send(c2, [(at(y, z, c, 0), at(y, z, c, xt)) for y, z, c, x in EVERY if x == 0])
        for xt in (1, 2, 3)
    ]
    c1, first = chain(
        [choose(x == 1), choose(x == 1)], spread[:1], [node_factors], [early_a], [[(1, 0)]], [None, (0, U)]
    )
    first = send(first, [(at(y, z, c, 1), at(y, z, c, 0)) for y, z, c, x in EVERY if x == 0])
    (modes,) = chain(
        [choose(x == 1, x == 2, x == 3), choose(x == 2, x == 3), choose(x % 2 == 1, x == 2)],
        [c1] + spread[1:], [node_factors, leaf_q], [early_a, early_b],
        [[(0, L), (3, 0)], [(0, L), (2, 0)]], [(1, 0)],
    )
    (modes,) = chain(
        [choose(x == 0, x != 0), choose(x == 0)], [first, modes], [leaf_q], [], [[(0, 0)]], [None],
    )
    return modes.T


def solution(mesh):
    return jax.shard_map(
        on_device,
        mesh=mesh,
        in_specs=(P(AXES, None), P(AXES, None), P()),
        out_specs=P(AXES, None),
        check_vma=False,
    )
```

```python
import jax
import jax.numpy as jnp
from jax import lax
from jax.experimental import pallas as pl
from jax.experimental.pallas import tpu as pltpu
from jax.sharding import PartitionSpec as P

AXES = ("wide", "narrow")
Y, Z, CORES, X = 4, 16, 2, 4
SNAPS, MODES = 512, 64


def at(y, z, core, x):
    return ((y * Z + z) * CORES + core) * X + x


EVERY = [(y, z, core, x) for y in range(Y) for z in range(Z) for core in range(CORES) for x in range(X)]


def split(value):
    high = value.astype(jnp.bfloat16)
    return high, (value - high.astype(jnp.float32)).astype(jnp.bfloat16)


def times(coefficient, factor):
    dims = (((1,), (1,)), ((), ()))
    c_high, c_low = split(coefficient)
    f_high, f_low = split(factor)
    both = lax.dot_general(
        jnp.concatenate([c_high, c_low], 0), f_high, dims, preferred_element_type=jnp.float32
    )
    cross = lax.dot_general(c_high, f_low, dims, preferred_element_type=jnp.float32)
    return both[:MODES] + (both[MODES:] + cross)


WORK_8, WORK_7 = 20 * 10**9, 20 * 10**9


def place():
    wide, x = lax.axis_index("wide"), lax.axis_index("narrow")
    return wide // (CORES * Z), (wide // CORES) % Z, wide % CORES, x


FACTOR = (SNAPS, SNAPS)
COEF = (MODES, SNAPS)
HBM, VMEM = pl.BlockSpec(memory_space=pltpu.HBM), pl.BlockSpec(memory_space=pltpu.VMEM)


def kernel_call(body, operands, near, outs, scratch, work=0, limit=12):
    return pl.pallas_call(
        body,
        out_shape=[
            pltpu.VMEM(shape, jnp.float32) if keep else jax.ShapeDtypeStruct(shape, jnp.float32)
            for shape, keep in outs
        ],
        in_specs=[VMEM if n else HBM for n in near],
        out_specs=[VMEM if keep else HBM for _, keep in outs],
        scratch_shapes=scratch,
        compiler_params=pltpu.CompilerParams(vmem_limit_bytes=limit << 20),
        cost_estimate=pl.CostEstimate(flops=work, bytes_accessed=0, transcendentals=0),
    )(*operands)


def half(ref, which):
    return ref.at[pl.ds(which * SNAPS, SNAPS), :]


def root_kernel(factors, basis, up, low, own, upper, other, held, sems):
    y, z, core, x = place()
    loads = [pltpu.make_async_copy(half(factors, h), half(own, h), sems.at[h]) for h in (0, 1)]
    root = (y == 2) & (z == 0) & (core == 0) & (x == 0)
    swap = (core == 1) & (x == 0)
    base = pltpu.make_async_copy(basis, held, sems.at[2])
    for load in loads:
        load.start()
    pl.when(root)(base.start)
    cut = pltpu.make_async_copy(half(own, 0), upper, sems.at[3])
    cut_up = pltpu.make_async_copy(half(own, 0), other, sems.at[4])
    cut_low = pltpu.make_async_copy(half(own, 1), other, sems.at[4])
    loads[0].wait()
    cut.start()
    pl.when(swap)(cut_up.start)
    loads[1].wait()
    pl.when(~swap)(cut_low.start)

    @pl.when(root)
    def _():
        base.wait()
        up[...] = times(held[...], own[:SNAPS, :])
        low[...] = times(held[...], own[SNAPS:, :])

    cut.wait()
    cut_low.wait()


def level_8_kernel(from_a, from_b, own, up, low):
    y, z, core, x = place()
    for y_here, coef in ((1, from_a), (3, from_b)):
        @pl.when((y == y_here) & (z == 0) & (core == 0) & (x == 0))
        def _():
            up[...] = times(coef[...], own[:SNAPS, :])
            low[...] = times(coef[...], own[SNAPS:, :])


def level_7_6_kernel(c_0, c_1, c_2, c_3, own, early_a, early_b, up, low, block, held, sem):
    y, z, core, x = place()
    for z_here, source, coefs in ((4, early_a, (c_0, c_2)), (12, early_b, (c_1, c_3))):
        @pl.when((z == z_here) & (core == 0) & (x == 0))
        def _():
            load = pltpu.make_async_copy(source, block, sem)
            load.start()
            for odd, coef in enumerate(coefs):
                @pl.when(y % 2 == odd)
                def _():
                    held[...] = coef[...]
            load.wait()
            held[...] = times(held[...], block[...])
            up[...] = times(held[...], own[:SNAPS, :])
            low[...] = times(held[...], own[SNAPS:, :])


def level_5_kernel(c_left, c_right, own, early_a, early_b, leaf, up, low, kept_a, kept_b, kept_leaf, sems):
    y, z, core, x = place()
    loads = [
        pltpu.make_async_copy(source, target, sems.at[i])
        for i, (source, target) in enumerate(((early_a, kept_a), (early_b, kept_b), (leaf, kept_leaf)))
    ]
    for load in loads:
        load.start()
    for z_here, coef in ((2, c_left), (6, c_right)):
        @pl.when((z % 8 == z_here) & (core == 0) & (x == 0))
        def _():
            up[...] = times(coef[...], own[:SNAPS, :])
            low[...] = times(coef[...], own[SNAPS:, :])
    for load in loads:
        load.wait()


def level_4_kernel(c_0, c_1, c_3, c_own, own, kept_a, early_c, out, held, block, sem):
    y, z, core, x = place()

    @pl.when((core == 0) & (x == 0))
    def _():
        is_late = (z == LATE[0]) | (z == LATE[1]) | (z == LATE[2])
        load = pltpu.make_async_copy(early_c, block, sem)
        pl.when(is_late)(load.start)
        for k, coef in ((0, c_0), (1, c_1), (3, c_3), (2, c_own)):
            @pl.when(z % 4 == k)
            def _():
                held[...] = coef[...]

        @pl.when(z % 2 == 1)
        def _():
            out[...] = times(held[...], own[SNAPS:, :])

        @pl.when(is_late)
        def _():
            load.wait()
            out[...] = times(held[...], block[...])

        @pl.when((z % 2 == 0) & ~is_late)
        def _():
            out[...] = times(held[...], kept_a[...])


def level_3_kernel(here, over, own, kept_a, kept_b, out):
    y, z, core, x = place()

    @pl.when((core == 1) & (x == 0))
    def _():
        out[...] = times(over[...], own[SNAPS:, :])

    @pl.when((core == 0) & (x == 0) & (z == 12))
    def _():
        out[...] = times(here[...], kept_a[...])

    @pl.when((core == 0) & (x == 0) & (z != 12))
    def _():
        out[...] = times(here[...], kept_b[...])


def level_2_kernel(coef, own, kept_a, keep, first):
    y, z, core, x = place()

    @pl.when(x == 1)
    def _():
        keep[...] = times(coef[...], kept_a[...])
        first[...] = times(keep[...], own[:SNAPS, :])


def leaf_kernel(c1, c2_x2, c2_x3, own, kept_a, kept_b, leaf, out, held):
    y, z, core, x = place()

    @pl.when(x == 1)
    def _():
        held[...] = times(c1[...], own[SNAPS:, :])

    @pl.when(x == 2)
    def _():
        held[...] = times(times(c2_x2[...], own[SNAPS:, :]), kept_a[...])

    @pl.when(x == 3)
    def _():
        held[...] = times(times(c2_x3[...], kept_b[...]), own[SNAPS:, :])

    @pl.when(x != 0)
    def _():
        out[...] = times(held[...], leaf[...])


def last_kernel(first, others, leaf, out):
    y, z, core, x = place()

    @pl.when(x == 0)
    def _():
        out[...] = times(first[...], leaf[...])

    @pl.when(x != 0)
    def _():
        out[...] = others[...]


LATE = (4, 6, 12)


def send(block, route):
    return lax.ppermute(block, AXES, route)


def on_device(node_factors, leaf_q, modal_basis):
    DMA = pltpu.SemaphoreType.DMA
    coef, block = pltpu.VMEM(COEF, jnp.float32), pltpu.VMEM(FACTOR, jnp.float32)

    up, low, own, upper, other = kernel_call(
        root_kernel, [node_factors, modal_basis.T], [0, 0],
        [(COEF, 1), (COEF, 1), (node_factors.shape, 1), (FACTOR, 0), (FACTOR, 0)], [coef, DMA((5,))],
        limit=56,
    )
    to_y1 = send(up, [(at(2, 0, 0, 0), at(1, 0, 0, 0))])
    to_y3 = send(low, [(at(2, 0, 0, 0), at(3, 0, 0, 0))])

    early_a = send(
        upper,
        [(at(y, z, c, x), at(y, z, c, x - 1)) for y, z, c, x in EVERY if x >= 2]
        + [(at(y, 8, 0, 0), at(y, 4, 0, 0)) for y in range(Y)]
        + [(at(y, z + 1, 0, 0), at(y, z, 0, 0)) for y in range(Y) for z in range(0, Z, 2) if z not in LATE]
        + [(at(y, 12, 1, 0), at(y, 12, 0, 0)) for y in range(Y)],
    )
    early_b = send(
        other,
        [(at(y, z, c, 2), at(y, z, c, 3)) for y, z, c, x in EVERY if x == 2]
        + [(at(y, 8, 0, 0), at(y, 12, 0, 0)) for y in range(Y)]
        + [(at(y, z, 1, 0), at(y, z, 0, 0)) for y in range(Y) for z in range(Z) if z != 12],
    )
    early_c = send(upper, [(at(y, z + 1, 0, 0), at(y, z, 0, 0)) for y in range(Y) for z in LATE])

    up, low = kernel_call(
        level_8_kernel, [to_y1, to_y3, own], [1, 1, 1], [(COEF, 1), (COEF, 1)], [], WORK_8
    )
    c7 = [
        send(block_, [(at(y, 0, 0, 0), at(y - 1 + k, zt, 0, 0)) for y in (1, 3)])
        for k, block_ in enumerate((up, low)) for zt in (4, 12)
    ]
    *c7, early_a, early_b = lax.optimization_barrier((*c7, early_a, early_b))
    up, low = kernel_call(
        level_7_6_kernel, [*c7, own, early_a, early_b], [1] * 5 + [0] * 2,
        [(COEF, 1), (COEF, 1)], [block, coef, DMA], WORK_7,
    )
    c5 = [
        send(block_, [(at(y, z, 0, 0), at(y, z + step, 0, 0)) for y in range(Y) for z in (4, 12)])
        for block_, step in ((up, -2), (low, 2))
    ]
    up, low, kept_a, kept_b, kept_leaf = kernel_call(
        level_5_kernel, [*c5, own, early_a, early_b, leaf_q], [1] * 3 + [0] * 3,
        [(COEF, 1), (COEF, 1)] + [(FACTOR, 1)] * 3, [DMA((3,))],
    )
    c4 = [
        send(block_, [(at(y, z, 0, 0), at(y, z + step, 0, 0)) for y in range(Y) for z in range(2, Z, 4)])
        for block_, step in ((up, -2), (up, -1), (low, 1))
    ]
    (c3,) = kernel_call(
        level_4_kernel, [*c4, low, own, kept_a, early_c], [1] * 6 + [0], [(COEF, 1)], [coef, block, DMA]
    )
    over = send(c3, [(at(y, z, 0, 0), at(y, z, 1, 0)) for y in range(Y) for z in range(Z)])
    (c2,) = kernel_call(level_3_kernel, [c3, over, own, kept_a, kept_b], [1] * 5, [(COEF, 1)], [])
    spread = [
        send(c2, [(at(y, z, c, 0), at(y, z, c, xt)) for y, z, c, x in EVERY if x == 0])
        for xt in (1, 2, 3)
    ]
    c1, first = kernel_call(
        level_2_kernel, [spread[0], own, kept_a], [1] * 3, [(COEF, 1), (COEF, 1)], []
    )
    first = send(first, [(at(y, z, c, 1), at(y, z, c, 0)) for y, z, c, x in EVERY if x == 0])
    (modes,) = kernel_call(
        leaf_kernel, [c1, *spread[1:], own, kept_a, kept_b, kept_leaf], [1] * 7, [(COEF, 1)], [coef]
    )
    (modes,) = pl.pallas_call(
        last_kernel,
        out_shape=[jax.ShapeDtypeStruct(COEF, jnp.float32)],
        in_specs=[VMEM] * 3,
        out_specs=[VMEM],
        compiler_params=pltpu.CompilerParams(vmem_limit_bytes=12 << 20),
    )(first, modes, kept_leaf)
    return modes.T


def solution(mesh):
    return jax.shard_map(
        on_device,
        mesh=mesh,
        in_specs=(P(AXES, None), P(AXES, None), P()),
        out_specs=P(AXES, None),
        check_vma=False,
    )
```

```python
import jax
import jax.numpy as jnp
from jax import lax
from jax.experimental import pallas as pl
from jax.experimental.pallas import tpu as pltpu
from jax.sharding import PartitionSpec as P

AXES = ("wide", "narrow")
Y, Z, CORES, X = 4, 16, 2, 4
SNAPS, MODES = 512, 64


def at(y, z, core, x):
    return ((y * Z + z) * CORES + core) * X + x


EVERY = [(y, z, core, x) for y in range(Y) for z in range(Z) for core in range(CORES) for x in range(X)]


def split(value):
    high = value.astype(jnp.bfloat16)
    return high, (value - high.astype(jnp.float32)).astype(jnp.bfloat16)


def times(coefficient, factor):
    dims = (((1,), (1,)), ((), ()))
    c_high, c_low = split(coefficient)
    f_high, f_low = split(factor)
    both = lax.dot_general(
        jnp.concatenate([c_high, c_low], 0), f_high, dims, preferred_element_type=jnp.float32
    )
    cross = lax.dot_general(c_high, f_low, dims, preferred_element_type=jnp.float32)
    return both[:MODES] + (both[MODES:] + cross)


WORK_8, WORK_7 = 0, 20 * 10**9


def place():
    wide, x = lax.axis_index("wide"), lax.axis_index("narrow")
    return wide // (CORES * Z), (wide // CORES) % Z, wide % CORES, x


FACTOR = (SNAPS, SNAPS)
COEF = (MODES, SNAPS)
HBM, VMEM = pl.BlockSpec(memory_space=pltpu.HBM), pl.BlockSpec(memory_space=pltpu.VMEM)


def kernel_call(body, operands, near, outs, scratch, work=0, limit=12):
    return pl.pallas_call(
        body,
        out_shape=[
            pltpu.VMEM(shape, jnp.float32) if keep else jax.ShapeDtypeStruct(shape, jnp.float32)
            for shape, keep in outs
        ],
        in_specs=[VMEM if n else HBM for n in near],
        out_specs=[VMEM if keep else HBM for _, keep in outs],
        scratch_shapes=scratch,
        compiler_params=pltpu.CompilerParams(vmem_limit_bytes=limit << 20),
        cost_estimate=pl.CostEstimate(flops=work, bytes_accessed=0, transcendentals=0),
    )(*operands)


def half(ref, which):
    return ref.at[pl.ds(which * SNAPS, SNAPS), :]


def cut_kernel(factors, own, upper, other, sems):
    y, z, core, x = place()
    middle = (z == 8) & (core == 0) & (x == 0)
    swap = middle | ((core == 1) & (x == 0))
    cut = pltpu.make_async_copy(half(factors, 0), upper, sems.at[0])
    cut_other = pltpu.make_async_copy(half(factors, 1), upper, sems.at[0])
    cut_up = pltpu.make_async_copy(half(factors, 0), other, sems.at[1])
    cut_low = pltpu.make_async_copy(half(factors, 1), other, sems.at[1])
    load = pltpu.make_async_copy(factors, own, sems.at[2])
    pl.when(middle)(cut_other.start)
    pl.when(~middle)(cut.start)
    pl.when(swap)(cut_up.start)
    pl.when(~swap)(cut_low.start)
    load.start()
    cut.wait()
    cut_low.wait()
    load.wait()


def root_kernel(basis, own, up, low, held, sem):
    y, z, core, x = place()

    @pl.when((y == 2) & (z == 0) & (core == 0) & (x == 0))
    def _():
        load = pltpu.make_async_copy(basis, held, sem)
        load.start()
        load.wait()
        up[...] = times(held[...], own[:SNAPS, :])
        low[...] = times(held[...], own[SNAPS:, :])


def level_8_kernel(from_a, from_b, own, up, low):
    y, z, core, x = place()
    for y_here, coef in ((1, from_a), (3, from_b)):
        @pl.when((y == y_here) & (z == 0) & (core == 0) & (x == 0))
        def _():
            up[...] = times(coef[...], own[:SNAPS, :])
            low[...] = times(coef[...], own[SNAPS:, :])


def level_7_6_kernel(c_0, c_1, c_2, c_3, own, early_a, early_b, up, low, block, held, sem):
    y, z, core, x = place()
    for z_here, source, coefs in ((4, early_b, (c_0, c_2)), (12, early_a, (c_1, c_3))):
        @pl.when((z == z_here) & (core == 0) & (x == 0))
        def _():
            load = pltpu.make_async_copy(source, block, sem)
            load.start()
            for odd, coef in enumerate(coefs):
                @pl.when(y % 2 == odd)
                def _():
                    held[...] = coef[...]
            load.wait()
            held[...] = times(held[...], block[...])
            up[...] = times(held[...], own[:SNAPS, :])
            low[...] = times(held[...], own[SNAPS:, :])


def level_5_kernel(c_left, c_right, own, early_a, early_b, leaf, up, low, kept_a, kept_b, kept_leaf, sems):
    y, z, core, x = place()
    loads = [
        pltpu.make_async_copy(source, target, sems.at[i])
        for i, (source, target) in enumerate(((early_a, kept_a), (early_b, kept_b), (leaf, kept_leaf)))
    ]
    for load in loads:
        load.start()
    for z_here, coef in ((2, c_left), (6, c_right)):
        @pl.when((z % 8 == z_here) & (core == 0) & (x == 0))
        def _():
            up[...] = times(coef[...], own[:SNAPS, :])
            low[...] = times(coef[...], own[SNAPS:, :])
    for load in loads:
        load.wait()


def level_4_kernel(c_0, c_1, c_3, c_own, own, kept_a, early_c, out, held, block, sem):
    y, z, core, x = place()

    @pl.when((core == 0) & (x == 0))
    def _():
        is_late = (z == LATE[0]) | (z == LATE[1]) | (z == LATE[2])
        load = pltpu.make_async_copy(early_c, block, sem)
        pl.when(is_late)(load.start)
        for k, coef in ((0, c_0), (1, c_1), (3, c_3), (2, c_own)):
            @pl.when(z % 4 == k)
            def _():
                held[...] = coef[...]

        @pl.when(z % 2 == 1)
        def _():
            out[...] = times(held[...], own[SNAPS:, :])

        @pl.when(is_late)
        def _():
            load.wait()
            out[...] = times(held[...], block[...])

        @pl.when((z % 2 == 0) & ~is_late)
        def _():
            out[...] = times(held[...], kept_a[...])


def level_3_kernel(here, over, own, kept_a, kept_b, out):
    y, z, core, x = place()

    @pl.when((core == 1) & (x == 0))
    def _():
        out[...] = times(over[...], own[SNAPS:, :])

    @pl.when((core == 0) & (x == 0) & (z == 4))
    def _():
        out[...] = times(here[...], kept_a[...])

    @pl.when((core == 0) & (x == 0) & (z != 4))
    def _():
        out[...] = times(here[...], kept_b[...])


def level_2_kernel(coef, own, kept_a, keep, first):
    y, z, core, x = place()

    @pl.when(x == 1)
    def _():
        keep[...] = times(coef[...], kept_a[...])
        first[...] = times(keep[...], own[:SNAPS, :])


def leaf_kernel(c1, c2_x2, c2_x3, own, kept_a, kept_b, leaf, out, held):
    y, z, core, x = place()

    @pl.when(x == 1)
    def _():
        held[...] = times(c1[...], own[SNAPS:, :])

    @pl.when(x == 2)
    def _():
        held[...] = times(times(c2_x2[...], own[SNAPS:, :]), kept_a[...])

    @pl.when(x == 3)
    def _():
        held[...] = times(times(c2_x3[...], kept_b[...]), own[SNAPS:, :])

    @pl.when(x != 0)
    def _():
        out[...] = times(held[...], leaf[...])


def last_kernel(first, others, leaf, out):
    y, z, core, x = place()

    @pl.when(x == 0)
    def _():
        out[...] = times(first[...], leaf[...])

    @pl.when(x != 0)
    def _():
        out[...] = others[...]


LATE = (4, 6, 12)


def send(block, route):
    return lax.ppermute(block, AXES, route)


def on_device(node_factors, leaf_q, modal_basis):
    DMA = pltpu.SemaphoreType.DMA
    coef, block = pltpu.VMEM(COEF, jnp.float32), pltpu.VMEM(FACTOR, jnp.float32)

    own, upper, other = kernel_call(
        cut_kernel, [node_factors], [0], [(node_factors.shape, 1), (FACTOR, 1), (FACTOR, 1)],
        [DMA((3,))], limit=56,
    )
    up, low = kernel_call(
        root_kernel, [modal_basis.T, own], [0, 1], [(COEF, 1), (COEF, 1)], [coef, DMA]
    )
    to_y1 = send(up, [(at(2, 0, 0, 0), at(1, 0, 0, 0))])
    to_y3 = send(low, [(at(2, 0, 0, 0), at(3, 0, 0, 0))])

    early_a = send(
        upper,
        [(at(y, z, c, x), at(y, z, c, x - 1)) for y, z, c, x in EVERY if x >= 2]
        + [(at(y, 8, 0, 0), at(y, 12, 0, 0)) for y in range(Y)]
        + [(at(y, z + 1, 0, 0), at(y, z, 0, 0)) for y in range(Y) for z in range(0, Z, 2) if z not in LATE]
        + [(at(y, 4, 1, 0), at(y, 4, 0, 0)) for y in range(Y)],
    )
    early_b = send(
        other,
        [(at(y, z, c, 2), at(y, z, c, 3)) for y, z, c, x in EVERY if x == 2]
        + [(at(y, 8, 0, 0), at(y, 4, 0, 0)) for y in range(Y)]
        + [(at(y, z, 1, 0), at(y, z, 0, 0)) for y in range(Y) for z in range(Z) if z != 4],
    )
    early_c = send(upper, [(at(y, z + 1, 0, 0), at(y, z, 0, 0)) for y in range(Y) for z in LATE])

    up, low = kernel_call(
        level_8_kernel, [to_y1, to_y3, own], [1, 1, 1], [(COEF, 1), (COEF, 1)], [], WORK_8
    )
    c7 = [
        send(block_, [(at(y, 0, 0, 0), at(y - 1 + k, zt, 0, 0)) for y in (1, 3)])
        for k, block_ in enumerate((up, low)) for zt in (4, 12)
    ]
    *c7, early_a, early_b = lax.optimization_barrier((*c7, early_a, early_b))
    up, low = kernel_call(
        level_7_6_kernel, [*c7, own, early_a, early_b], [1] * 5 + [0] * 2,
        [(COEF, 1), (COEF, 1)], [block, coef, DMA], WORK_7,
    )
    c5 = [
        send(block_, [(at(y, z, 0, 0), at(y, z + step, 0, 0)) for y in range(Y) for z in (4, 12)])
        for block_, step in ((up, -2), (low, 2))
    ]
    up, low, kept_a, kept_b, kept_leaf = kernel_call(
        level_5_kernel, [*c5, own, early_a, early_b, leaf_q], [1] * 3 + [0] * 3,
        [(COEF, 1), (COEF, 1)] + [(FACTOR, 1)] * 3, [DMA((3,))],
    )
    c4 = [
        send(block_, [(at(y, z, 0, 0), at(y, z + step, 0, 0)) for y in range(Y) for z in range(2, Z, 4)])
        for block_, step in ((up, -2), (up, -1), (low, 1))
    ]
    (c3,) = kernel_call(
        level_4_kernel, [*c4, low, own, kept_a, early_c], [1] * 6 + [0], [(COEF, 1)], [coef, block, DMA]
    )
    over = send(c3, [(at(y, z, 0, 0), at(y, z, 1, 0)) for y in range(Y) for z in range(Z)])
    (c2,) = kernel_call(level_3_kernel, [c3, over, own, kept_a, kept_b], [1] * 5, [(COEF, 1)], [])
    spread = [
        send(c2, [(at(y, z, c, 0), at(y, z, c, xt)) for y, z, c, x in EVERY if x == 0])
        for xt in (1, 2, 3)
    ]
    c1, first = kernel_call(
        level_2_kernel, [spread[0], own, kept_a], [1] * 3, [(COEF, 1), (COEF, 1)], []
    )
    first = send(first, [(at(y, z, c, 1), at(y, z, c, 0)) for y, z, c, x in EVERY if x == 0])
    (modes,) = kernel_call(
        leaf_kernel, [c1, *spread[1:], own, kept_a, kept_b, kept_leaf], [1] * 7, [(COEF, 1)], [coef]
    )
    (modes,) = pl.pallas_call(
        last_kernel,
        out_shape=[jax.ShapeDtypeStruct(COEF, jnp.float32)],
        in_specs=[VMEM] * 3,
        out_specs=[VMEM],
        compiler_params=pltpu.CompilerParams(vmem_limit_bytes=12 << 20),
    )(first, modes, kept_leaf)
    return modes.T


def solution(mesh):
    return jax.shard_map(
        on_device,
        mesh=mesh,
        in_specs=(P(AXES, None), P(AXES, None), P()),
        out_specs=P(AXES, None),
        check_vma=False,
    )
```

```python
import jax
import jax.numpy as jnp
from jax import lax
from jax.experimental import pallas as pl
from jax.experimental.pallas import tpu as pltpu
from jax.sharding import PartitionSpec as P

AXES = ("wide", "narrow")
Y, Z, CORES, X = 4, 16, 2, 4
SNAPS, MODES = 512, 64


def at(y, z, core, x):
    return ((y * Z + z) * CORES + core) * X + x


EVERY = [(y, z, core, x) for y in range(Y) for z in range(Z) for core in range(CORES) for x in range(X)]


def split(value):
    high = value.astype(jnp.bfloat16)
    return high, (value - high.astype(jnp.float32)).astype(jnp.bfloat16)


def times(coefficient, factor):
    dims = (((1,), (1,)), ((), ()))
    c_high, c_low = split(coefficient)
    f_high, f_low = split(factor)
    both = lax.dot_general(
        jnp.concatenate([c_high, c_low], 0), f_high, dims, preferred_element_type=jnp.float32
    )
    cross = lax.dot_general(c_high, f_low, dims, preferred_element_type=jnp.float32)
    return both[:MODES] + (both[MODES:] + cross)


WORK_8, WORK_7, WORK_5 = 0, 3 * 10**9, 0


def place():
    wide, x = lax.axis_index("wide"), lax.axis_index("narrow")
    return wide // (CORES * Z), (wide // CORES) % Z, wide % CORES, x


FACTOR = (SNAPS, SNAPS)
COEF = (MODES, SNAPS)
HBM, VMEM = pl.BlockSpec(memory_space=pltpu.HBM), pl.BlockSpec(memory_space=pltpu.VMEM)


def kernel_call(body, operands, near, outs, scratch, work=0, limit=12):
    return pl.pallas_call(
        body,
        out_shape=[
            pltpu.VMEM(shape, jnp.float32) if keep else jax.ShapeDtypeStruct(shape, jnp.float32)
            for shape, keep in outs
        ],
        in_specs=[VMEM if n else HBM for n in near],
        out_specs=[VMEM for _ in outs],
        scratch_shapes=scratch,
        compiler_params=pltpu.CompilerParams(vmem_limit_bytes=limit << 20),
        cost_estimate=pl.CostEstimate(flops=work, bytes_accessed=0, transcendentals=0),
    )(*operands)


def half(ref, which):
    return ref.at[pl.ds(which * SNAPS, SNAPS), :]


def cut_kernel(factors, upper, other, sems):
    y, z, core, x = place()
    swap = (core == 1) & (x == 0)
    cut = pltpu.make_async_copy(half(factors, 0), upper, sems.at[0])
    cut_up = pltpu.make_async_copy(half(factors, 0), other, sems.at[1])
    cut_low = pltpu.make_async_copy(half(factors, 1), other, sems.at[1])
    cut.start()
    pl.when(swap)(cut_up.start)
    pl.when(~swap)(cut_low.start)
    cut.wait()
    cut_low.wait()


def root_kernel(basis, upper, other, up, low):
    y, z, core, x = place()

    @pl.when((y == 2) & (z == 0) & (core == 0) & (x == 0))
    def _():
        up[...] = times(basis[...], upper[...])
        low[...] = times(basis[...], other[...])


def level_8_kernel(from_a, from_b, upper, other, up, low):
    y, z, core, x = place()
    for y_here, coef in ((1, from_a), (3, from_b)):
        @pl.when((y == y_here) & (z == 0) & (core == 0) & (x == 0))
        def _():
            low[...] = times(coef[...], other[...])
            up[...] = times(coef[...], upper[...])


def level_7_6_kernel(c4_odd, c4_even, c12_odd, c12_even, own, early_a, early_b, up, low, held):
    y, z, core, x = place()
    for z_here, source, coefs in ((4, early_a, (c4_even, c4_odd)), (12, early_b, (c12_even, c12_odd))):
        @pl.when((z == z_here) & (core == 0) & (x == 0))
        def _():
            for odd, coef in enumerate(coefs):
                @pl.when(y % 2 == odd)
                def _():
                    held[...] = coef[...]
            held[...] = times(held[...], source[...])
            up[...] = times(held[...], own[:SNAPS, :])
            low[...] = times(held[...], own[SNAPS:, :])


def level_5_kernel(c_left, c_right, own, up, low):
    y, z, core, x = place()
    for z_here, coef in ((2, c_left), (6, c_right)):
        @pl.when((z % 8 == z_here) & (core == 0) & (x == 0))
        def _():
            up[...] = times(coef[...], own[:SNAPS, :])
            low[...] = times(coef[...], own[SNAPS:, :])


def level_4_kernel(c_0, c_1, c_3, c_own, own, early_a, early_c, early_d, out, held):
    y, z, core, x = place()

    @pl.when((core == 0) & (x == 0))
    def _():
        is_late = (z == LATE[0]) | (z == LATE[1]) | (z == LATE[2])
        for k, coef in ((0, c_0), (1, c_1), (3, c_3), (2, c_own)):
            @pl.when(z % 4 == k)
            def _():
                held[...] = coef[...]

        @pl.when(z % 2 == 1)
        def _():
            out[...] = times(held[...], own[SNAPS:, :])

        @pl.when(is_late)
        def _():
            out[...] = times(held[...], early_c[...])

        @pl.when((z % 2 == 0) & ~is_late)
        def _():
            out[...] = times(held[...], early_a[...])


def level_3_kernel(here, over, own, early_a, early_b, out):
    y, z, core, x = place()

    @pl.when((core == 1) & (x == 0))
    def _():
        out[...] = times(over[...], own[SNAPS:, :])

    @pl.when((core == 0) & (x == 0) & (z == 12))
    def _():
        out[...] = times(here[...], early_a[...])

    @pl.when((core == 0) & (x == 0) & (z != 12))
    def _():
        out[...] = times(here[...], early_b[...])


def leaf_kernel(c2, c2_x1, c2_x2, c2_x3, own, early_a, early_b, early_d, early_e, leaf, out, held):
    y, z, core, x = place()

    for source, mine in ((early_a, (core == 1) | (z % 2 == 1)), (early_d, (core == 0) & (z % 2 == 0))):
        @pl.when((x == 0) & mine)
        def _():
            held[...] = times(times(c2[...], early_e[...]), source[...])

    @pl.when(x == 1)
    def _():
        held[...] = times(times(c2_x1[...], early_a[...]), own[SNAPS:, :])

    @pl.when(x == 2)
    def _():
        held[...] = times(times(c2_x2[...], own[SNAPS:, :]), early_a[...])

    @pl.when(x == 3)
    def _():
        held[...] = times(times(c2_x3[...], early_b[...]), own[SNAPS:, :])

    out[...] = times(held[...], leaf[...])


LATE = (4, 6, 12)


def send(block, route):
    return lax.ppermute(block, AXES, route)


def on_device(node_factors, leaf_q, modal_basis):
    DMA = pltpu.SemaphoreType.DMA
    coef, block = pltpu.VMEM(COEF, jnp.float32), pltpu.VMEM(FACTOR, jnp.float32)

    upper, other = kernel_call(
        cut_kernel, [node_factors], [0], [(FACTOR, 1), (FACTOR, 1)], [DMA((2,))], limit=58
    )
    up, low = kernel_call(root_kernel, [modal_basis.T, upper, other], [1] * 3, [(COEF, 1), (COEF, 1)], [])
    to_y1 = send(up, [(at(2, 0, 0, 0), at(1, 0, 0, 0))])
    to_y3 = send(low, [(at(2, 0, 0, 0), at(3, 0, 0, 0))])

    early_a = send(
        upper,
        [(at(y, z, c, x), at(y, z, c, x - 1)) for y, z, c, x in EVERY if x >= 2]
        + [(at(y, 8, 0, 0), at(y, 4, 0, 0)) for y in range(Y)]
        + [(at(y, z + 1, 0, 0), at(y, z, 0, 0)) for y in range(Y) for z in range(0, Z, 2) if z not in LATE]
        + [(at(y, 12, 1, 0), at(y, 12, 0, 0)) for y in range(Y)]
        + [(at(y, z, c, 1), at(y, z, c, 0)) for y, z, c, x in EVERY if x == 1 and (c == 1 or z % 2 == 1)],
    )
    early_b = send(
        other,
        [(at(y, z, c, 2), at(y, z, c, 3)) for y, z, c, x in EVERY if x == 2]
        + [(at(y, 8, 0, 0), at(y, 12, 0, 0)) for y in range(Y)]
        + [(at(y, z, 1, 0), at(y, z, 0, 0)) for y in range(Y) for z in range(Z) if z != 12],
    )
    early_d = send(upper, [(at(y, z, 0, 1), at(y, z, 0, 0)) for y in range(Y) for z in range(0, Z, 2)])
    early_e = send(upper, [(at(y, z, c, 2), at(y, z, c, 0)) for y, z, c, x in EVERY if x == 2])

    up, low = kernel_call(
        level_8_kernel, [to_y1, to_y3, upper, other], [1] * 4, [(COEF, 1), (COEF, 1)], [], WORK_8
    )
    c7 = [
        send(block_, [(at(y, 0, 0, 0), at(y - 1 + k, zt, 0, 0)) for y in (1, 3)])
        for zt in (4, 12) for k, block_ in ((1, low), (0, up))
    ]
    *c7, upper = lax.optimization_barrier((*c7, upper))
    early_c = send(upper, [(at(y, z + 1, 0, 0), at(y, z, 0, 0)) for y in range(Y) for z in LATE])
    *c7, early_a, early_b = lax.optimization_barrier((*c7, early_a, early_b))
    up, low = kernel_call(
        level_7_6_kernel, [*c7, node_factors, early_a, early_b], [1] * 7, [(COEF, 1), (COEF, 1)], [coef], WORK_7
    )
    c5 = [
        send(block_, [(at(y, z, 0, 0), at(y, z + step, 0, 0)) for y in range(Y) for z in (4, 12)])
        for block_, step in ((up, -2), (low, 2))
    ]
    up, low = kernel_call(
        level_5_kernel, [*c5, node_factors], [1] * 3, [(COEF, 1), (COEF, 1)], [], WORK_5
    )
    c4 = [
        send(block_, [(at(y, z, 0, 0), at(y, z + step, 0, 0)) for y in range(Y) for z in range(2, Z, 4)])
        for block_, step in ((up, -2), (up, -1), (low, 1))
    ]
    (c3,) = kernel_call(
        level_4_kernel, [*c4, low, node_factors, early_a, early_c, early_d], [1] * 7 + [0], [(COEF, 1)], [coef]
    )
    over = send(c3, [(at(y, z, 0, 0), at(y, z, 1, 0)) for y in range(Y) for z in range(Z)])
    (c2,) = kernel_call(
        level_3_kernel, [c3, over, node_factors, early_a, early_b], [1] * 5, [(COEF, 1)], []
    )
    spread = [
        send(c2, [(at(y, z, c, 0), at(y, z, c, xt)) for y, z, c, x in EVERY if x == 0])
        for xt in (1, 2, 3)
    ]
    (modes,) = kernel_call(
        leaf_kernel, [c2, *spread, node_factors, early_a, early_b, early_d, early_e, leaf_q], [1] * 10,
        [(COEF, 0)], [coef],
    )
    return modes.T


def solution(mesh):
    return jax.shard_map(
        on_device,
        mesh=mesh,
        in_specs=(P(AXES, None), P(AXES, None), P()),
        out_specs=P(AXES, None),
        check_vma=False,
    )
```

```python
import jax
import jax.numpy as jnp
from jax import lax
from jax.experimental import pallas as pl
from jax.experimental.pallas import tpu as pltpu
from jax.sharding import PartitionSpec as P

AXES = ("wide", "narrow")
Y, Z, CORES, X = 4, 16, 2, 4
SNAPS, MODES = 512, 64


def at(y, z, core, x):
    return ((y * Z + z) * CORES + core) * X + x


EVERY = [(y, z, core, x) for y in range(Y) for z in range(Z) for core in range(CORES) for x in range(X)]


def split(value):
    high = value.astype(jnp.bfloat16)
    return high, (value - high.astype(jnp.float32)).astype(jnp.bfloat16)


def times(coefficient, factor):
    dims = (((1,), (1,)), ((), ()))
    c_high, c_low = split(coefficient)
    f_high, f_low = split(factor)
    both = lax.dot_general(
        jnp.concatenate([c_high, c_low], 0), f_high, dims, preferred_element_type=jnp.float32
    )
    cross = lax.dot_general(c_high, f_low, dims, preferred_element_type=jnp.float32)
    return both[:MODES] + (both[MODES:] + cross)


WORK_8, WORK_7, WORK_5 = 0, 3 * 10**9, 7 * 10**9


def place():
    wide, x = lax.axis_index("wide"), lax.axis_index("narrow")
    return wide // (CORES * Z), (wide // CORES) % Z, wide % CORES, x


FACTOR = (SNAPS, SNAPS)
COEF = (MODES, SNAPS)
HBM, VMEM = pl.BlockSpec(memory_space=pltpu.HBM), pl.BlockSpec(memory_space=pltpu.VMEM)


def kernel_call(body, operands, near, outs, scratch, work=0, limit=12):
    return pl.pallas_call(
        body,
        out_shape=[
            pltpu.VMEM(shape, jnp.float32) if keep else jax.ShapeDtypeStruct(shape, jnp.float32)
            for shape, keep in outs
        ],
        in_specs=[VMEM if n else HBM for n in near],
        out_specs=[VMEM for _ in outs],
        scratch_shapes=scratch,
        compiler_params=pltpu.CompilerParams(vmem_limit_bytes=limit << 20),
        cost_estimate=pl.CostEstimate(flops=work, bytes_accessed=0, transcendentals=0),
    )(*operands)


def half(ref, which):
    return ref.at[pl.ds(which * SNAPS, SNAPS), :]


def cut_kernel(factors, upper, other, sems):
    y, z, core, x = place()
    swap = (core == 1) & (x == 0)
    cut = pltpu.make_async_copy(half(factors, 0), upper, sems.at[0])
    cut_up = pltpu.make_async_copy(half(factors, 0), other, sems.at[1])
    cut_low = pltpu.make_async_copy(half(factors, 1), other, sems.at[1])
    cut.start()
    pl.when(swap)(cut_up.start)
    pl.when(~swap)(cut_low.start)
    cut.wait()
    cut_low.wait()


def root_kernel(basis, upper, other, up, low):
    y, z, core, x = place()

    @pl.when((y == 2) & (z == 0) & (core == 0) & (x == 0))
    def _():
        up[...] = times(basis[...], upper[...])
        low[...] = times(basis[...], other[...])


def level_8_kernel(from_a, from_b, upper, other, up, low, up_far, low_far):
    y, z, core, x = place()
    for y_here, coef in ((1, from_a), (3, from_b)):
        @pl.when((y == y_here) & (z == 0) & (core == 0) & (x == 0))
        def _():
            low[...] = times(coef[...], other[...])
            up[...] = times(coef[...], upper[...])
            low_far[...] = low[...]
            up_far[...] = up[...]


def level_7_6_kernel(c4_odd, c4_even, c12_odd, c12_even, own, early_a, early_b, up, low, held):
    y, z, core, x = place()
    for z_here, source, coefs in ((4, early_a, (c4_even, c4_odd)), (12, early_b, (c12_even, c12_odd))):
        @pl.when((z == z_here) & (core == 0) & (x == 0))
        def _():
            for odd, coef in enumerate(coefs):
                @pl.when(y % 2 == odd)
                def _():
                    held[...] = coef[...]
            held[...] = times(held[...], source[...])
            up[...] = times(held[...], own[:SNAPS, :])
            low[...] = times(held[...], own[SNAPS:, :])


def level_5_kernel(c_left, c_right, own, up, low):
    y, z, core, x = place()
    for z_here, coef in ((2, c_left), (6, c_right)):
        @pl.when((z % 8 == z_here) & (core == 0) & (x == 0))
        def _():
            up[...] = times(coef[...], own[:SNAPS, :])
            low[...] = times(coef[...], own[SNAPS:, :])


def level_4_kernel(c_0, c_1, c_3, c_own, own, early_a, early_c, out, held):
    y, z, core, x = place()

    @pl.when((core == 0) & (x == 0))
    def _():
        is_late = (z == LATE[0]) | (z == LATE[1]) | (z == LATE[2])
        for k, coef in ((0, c_0), (1, c_1), (3, c_3), (2, c_own)):
            @pl.when(z % 4 == k)
            def _():
                held[...] = coef[...]

        @pl.when(z % 2 == 1)
        def _():
            out[...] = times(held[...], own[SNAPS:, :])

        @pl.when(is_late)
        def _():
            out[...] = times(held[...], early_c[...])

        @pl.when((z % 2 == 0) & ~is_late)
        def _():
            out[...] = times(held[...], early_a[...])


def level_3_kernel(here, over, own, early_a, early_b, out):
    y, z, core, x = place()

    @pl.when((core == 1) & (x == 0))
    def _():
        out[...] = times(over[...], own[SNAPS:, :])

    @pl.when((core == 0) & (x == 0) & (z == 12))
    def _():
        out[...] = times(here[...], early_a[...])

    @pl.when((core == 0) & (x == 0) & (z != 12))
    def _():
        out[...] = times(here[...], early_b[...])


def pair_kernel(upper, early_a, out):
    y, z, core, x = place()

    @pl.when(x == 1)
    def _():
        a_high, a_low = split(upper[...])
        b_high, b_low = split(early_a[...])
        dot = lambda a, b: jnp.dot(a, b, preferred_element_type=jnp.float32)
        out[...] = dot(a_high, b_high) + (dot(a_high, b_low) + dot(a_low, b_high))


def leaf_kernel(c2, c2_x1, c2_x2, c2_x3, own, early_a, early_b, pair, leaf, out, held):
    y, z, core, x = place()

    @pl.when(x == 0)
    def _():
        held[...] = times(c2[...], pair[...])

    @pl.when(x == 1)
    def _():
        held[...] = times(times(c2_x1[...], early_a[...]), own[SNAPS:, :])

    @pl.when(x == 2)
    def _():
        held[...] = times(times(c2_x2[...], own[SNAPS:, :]), early_a[...])

    @pl.when(x == 3)
    def _():
        held[...] = times(times(c2_x3[...], early_b[...]), own[SNAPS:, :])

    out[...] = times(held[...], leaf[...])


LATE = (4, 6, 12)


def send(block, route):
    return lax.ppermute(block, AXES, route)


def on_device(node_factors, leaf_q, modal_basis):
    DMA = pltpu.SemaphoreType.DMA
    coef, block = pltpu.VMEM(COEF, jnp.float32), pltpu.VMEM(FACTOR, jnp.float32)

    upper, other = kernel_call(
        cut_kernel, [node_factors], [0], [(FACTOR, 1), (FACTOR, 1)], [DMA((2,))], limit=58
    )
    up, low = kernel_call(root_kernel, [modal_basis.T, upper, other], [1] * 3, [(COEF, 1), (COEF, 1)], [])
    to_y1 = send(up, [(at(2, 0, 0, 0), at(1, 0, 0, 0))])
    to_y3 = send(low, [(at(2, 0, 0, 0), at(3, 0, 0, 0))])

    early_a = send(
        upper,
        [(at(y, z, c, x), at(y, z, c, x - 1)) for y, z, c, x in EVERY if x >= 2]
        + [(at(y, 8, 0, 0), at(y, 4, 0, 0)) for y in range(Y)]
        + [(at(y, z + 1, 0, 0), at(y, z, 0, 0)) for y in range(Y) for z in range(0, Z, 2) if z not in LATE]
        + [(at(y, 12, 1, 0), at(y, 12, 0, 0)) for y in range(Y)],
    )
    early_b = send(
        other,
        [(at(y, z, c, 2), at(y, z, c, 3)) for y, z, c, x in EVERY if x == 2]
        + [(at(y, 8, 0, 0), at(y, 12, 0, 0)) for y in range(Y)]
        + [(at(y, z, 1, 0), at(y, z, 0, 0)) for y in range(Y) for z in range(Z) if z != 12],
    )

    up, low, up_far, low_far = kernel_call(
        level_8_kernel, [to_y1, to_y3, upper, other], [1] * 4, [(COEF, 1)] * 4, [], WORK_8
    )
    c7 = [
        send(block_, [(at(y, 0, 0, 0), at(y - 1 + k, zt, 0, 0)) for y in (1, 3)])
        for zt, k, block_ in ((4, 1, low), (4, 0, up), (12, 1, low_far), (12, 0, up_far))
    ]
    *c7, upper = lax.optimization_barrier((*c7, upper))
    early_c = send(upper, [(at(y, z + 1, 0, 0), at(y, z, 0, 0)) for y in range(Y) for z in LATE])
    *c7, early_a, early_b = lax.optimization_barrier((*c7, early_a, early_b))
    up, low = kernel_call(
        level_7_6_kernel, [*c7, node_factors, early_a, early_b], [1] * 7, [(COEF, 1), (COEF, 1)], [coef], WORK_7
    )
    early_x, up, low = lax.optimization_barrier((early_a, up, low))
    (pair,) = kernel_call(pair_kernel, [upper, early_x], [1] * 2, [(FACTOR, 1)], [])
    pair = send(pair, [(at(y, z, c, 1), at(y, z, c, 0)) for y, z, c, x in EVERY if x == 1])
    c5 = [
        send(block_, [(at(y, z, 0, 0), at(y, z + step, 0, 0)) for y in range(Y) for z in (4, 12)])
        for block_, step in ((up, -2), (low, 2))
    ]
    up, low = kernel_call(
        level_5_kernel, [*c5, node_factors], [1] * 3, [(COEF, 1), (COEF, 1)], [], WORK_5
    )
    c4 = [
        send(block_, [(at(y, z, 0, 0), at(y, z + step, 0, 0)) for y in range(Y) for z in range(2, Z, 4)])
        for block_, step in ((up, -2), (up, -1), (low, 1))
    ]
    (c3,) = kernel_call(
        level_4_kernel, [*c4, low, node_factors, early_a, early_c], [1] * 7, [(COEF, 1)], [coef]
    )
    over = send(c3, [(at(y, z, 0, 0), at(y, z, 1, 0)) for y in range(Y) for z in range(Z)])
    (c2,) = kernel_call(
        level_3_kernel, [c3, over, node_factors, early_a, early_b], [1] * 5, [(COEF, 1)], []
    )
    spread = [
        send(c2, [(at(y, z, c, 0), at(y, z, c, xt)) for y, z, c, x in EVERY if x == 0])
        for xt in (1, 2, 3)
    ]
    (modes,) = kernel_call(
        leaf_kernel, [c2, *spread, node_factors, early_a, early_b, pair, leaf_q], [1] * 9,
        [(COEF, 0)], [coef],
    )
    return modes.T


def solution(mesh):
    return jax.shard_map(
        on_device,
        mesh=mesh,
        in_specs=(P(AXES, None), P(AXES, None), P()),
        out_specs=P(AXES, None),
        check_vma=False,
    )
```
